128 devices in a mesh: row: 8 (over y, x_hi), col: 16 (over x_lo, z, core).
Axes of the slice: x: 4 (x_hi: 2, x_lo: 2; x = x_hi * 2 + x_lo), y: 4, z: 4, core: 2. Of those that a mesh axis runs over, the one named last changes fastest.
Arguments:
- coef_occ: bfloat16 [16384, 2560], P('row', 'col'), may hold values from -6 to 6
- coef_resp: bfloat16 [16384, 2560], P('col', 'row'), may hold values from -0.125 to 0.125
- orb_energy: float32 [2560], P('col'), may hold values from -2 to -0.3
- lap_index: int32 [1], replicated, may hold values from 0 to 7
- density_mask: int32 [128, 128], P('row', 'col'), may hold values 0 or 1
- tri_blocks: bfloat16 [8, 64, 128, 128], P('row'), may hold values from -0.5 to 0.5
- block_ao: int32 [8, 64], P('row'), may hold values from 0 to 15
- block_slab: int32 [8, 64], P('row'), may hold values from 0 to 15
- metric: bfloat16 [2048, 128], P('col'), may hold values from -0.1875 to 0.1875
Outputs:
- pseudo: bfloat16 [16384, 16384], P('row', 'col')
- ri_grad: bfloat16 [16384, 2048], P('row', 'col')
The draws below stay inside these ranges and needn't reach their ends.
All inputs are finite; a program needn't handle non-finite values. No bound on the sum of `density_mask` on one device may be relied on, other than what follows from the above.
Results may differ from the reference program's by a relative error of at most 0.014.
Values may be sent and summed in bfloat16 or wider, within the bound.
No kernel may reach another device: no remote copies, remote signals or barrier semaphores. Data moves between devices by JAX's collectives and lax.ppermute only.
A program may use at most 192 MiB of HBM per device.

```python
import math
import jax
import jax.numpy as jnp
from jax import lax

NAO = 16384
NOCC = 2560
RQ = 128
NBL = 64
NB = 128
N_ROW = 8
N_COL = 16


def touch_ends(result, stream_key, smallest, top_value):
    longest = result.shape.index(max(result.shape))
    spots = []
    for shift in (0, 1):
        where = [jax.random.randint(jax.random.fold_in(stream_key, axis), (), 0, length) for axis, length in enumerate(result.shape)]
        where[longest] = (where[longest] + shift) % result.shape[longest]
        spots.append(tuple(where))
    return result.at[spots[0]].set(smallest).at[spots[1]].set(top_value)


def level_of(own_key, extent, shards, low, largest):
    factor_of, own = 1.0, jax.random.fold_in(own_key, 6)
    for dim, parts in shards:
        steps = jnp.exp(jax.random.uniform(jax.random.fold_in(own, dim), (parts,), jnp.float32, low / len(shards), largest / len(shards)))
        factor_of = factor_of * jnp.repeat(steps, extent[dim] // parts).reshape([-1 if axis == dim else 1 for axis in range(len(extent))])
    return factor_of


def scatter_about(key, shape, scale, reach, cuts=(), kind=jnp.bfloat16):
    entries = scale * jax.random.normal(key, shape, jnp.float32)
    if cuts:
        entries = entries * level_of(key, shape, cuts, -0.22, 0.18)
    return jnp.clip(entries, -reach, reach).astype(kind)


def setup_inputs(seed: int = 0) -> dict:
    key_of = jax.random.split(jax.random.key(seed), 10)
    coef_occ = scatter_about(key_of[0], (NAO, NOCC), 1.0, 6.0, ((0, 8), (1, 16)))
    coef_resp = scatter_about(key_of[1], (NAO, NOCC), NOCC ** -0.5, 0.125, ((0, 16), (1, 8)))
    orb_energy = jnp.clip(-2.0 + 1.7 * jax.random.uniform(key_of[2], (NOCC,), jnp.float32) ** level_of(key_of[2], (NOCC,), ((0, 16),), -0.2, 0.2), -2.0, -0.3)
    lap_index = jax.random.randint(key_of[3], (1,), 0, 8).astype(jnp.int32)
    density_mask = touch_ends((jax.random.randint(key_of[4], (NB, NB), 0, 2) < 1).astype(jnp.int32), jax.random.fold_in(key_of[4], 1), 0, 1)
    tri_blocks = scatter_about(key_of[5], (N_ROW, NBL, 128, RQ), 128 ** -0.5, 0.5, ((0, 8),))
    block_ao = touch_ends(jax.random.randint(key_of[6], (N_ROW, NBL), 0, NB // N_ROW), jax.random.fold_in(key_of[6], 1), 0, (NB // N_ROW) - 1).astype(jnp.int32)
    block_slab = touch_ends(jax.random.randint(key_of[7], (N_ROW, NBL), 0, N_COL), jax.random.fold_in(key_of[7], 1), 0, N_COL - 1).astype(jnp.int32)
    metric = scatter_about(key_of[8], (N_COL * RQ, RQ), (RQ * N_ROW) ** -0.5, 0.1875, ((0, 16),))
    return {"coef_occ": coef_occ, "coef_resp": coef_resp, "orb_energy": orb_energy, "lap_index": lap_index, "density_mask": density_mask, "tri_blocks": tri_blocks, "block_ao": block_ao, "block_slab": block_slab, "metric": metric}


def reference(coef_occ, coef_resp, orb_energy, lap_index, density_mask, tri_blocks, block_ao, block_slab, metric):
    t_point = 0.04 * jnp.exp(0.5 * math.log(2.0) * lap_index[0].astype(jnp.float32))
    weighted = (coef_occ.astype(jnp.float32) * jnp.exp(t_point * orb_energy)[None, :]).astype(jnp.bfloat16)
    lanes = NAO // 1024

    def density_rows(inputs):
        rows_w, rows_m = inputs
        product = jnp.dot(rows_w, coef_resp.T, preferred_element_type=jnp.float32)
        spread = jnp.repeat(jnp.repeat(rows_m.astype(jnp.float32), 128, 0), 128, 1)
        return (product * spread).astype(jnp.bfloat16)

    pseudo = lax.map(density_rows, (weighted.reshape(lanes, 1024, NOCC), density_mask.reshape(lanes, 8, NB))).reshape(NAO, NAO)
    row_len = NAO // N_ROW
    slab_ids = jnp.arange(N_COL, dtype=jnp.int32)
    metric_f = metric.reshape(N_COL, RQ, RQ).astype(jnp.float32)

    def per_row(carry, inputs):
        prow, tri, aos, slabs = inputs
        picked = prow.reshape(row_len // 128, 128, NAO)[aos]
        partial_value = jnp.einsum('bmq,bmc->bqc', tri.astype(jnp.float32), picked.astype(jnp.float32))
        owner = (slabs[None, :] == slab_ids[:, None]).astype(jnp.float32)
        slab_sum = jnp.einsum('sb,bqc->sqc', owner, partial_value, precision=lax.Precision.HIGHEST).astype(jnp.bfloat16)
        term = jnp.einsum('spm,sqp->msq', slab_sum.astype(jnp.float32), metric_f, precision=lax.Precision.HIGHEST)
        return carry + term.reshape(NAO, N_COL * RQ), None

    start = jnp.zeros((NAO, N_COL * RQ), jnp.float32)
    total, unused = lax.scan(per_row, start, (pseudo.reshape(N_ROW, row_len, NAO), tri_blocks, block_ao, block_slab))
    return pseudo, total.astype(jnp.bfloat16)
```

```python
import functools
import math

import jax
import jax.numpy as jnp
from jax import lax
from jax.experimental import pallas as pl
from jax.experimental.pallas import tpu as pltpu
from jax.sharding import PartitionSpec as P

N_ROW = 8
N_COL = 16
BOTH = ("row", "col")


def send(x, to):
    pairs = []
    for r in range(N_ROW):
        for c in range(N_COL):
            rr, cc = to(r, c)
            pairs.append((r * N_COL + c, rr * N_COL + cc))
    return lax.ppermute(x, BOTH, pairs)


def along_y(step):
    return lambda r, c: ((r + 2 * step) % N_ROW, c)


def flip_x(r, c):
    return r ^ 1, c


def owner_of(j):
    return lambda r, c: (c // 2, (r // 2) * 4 + ((2 * (r % 2) + c % 2) ^ j))


def slab_kernel(first, ao, slab_at, tri_ref, pseudo_ref, *outs):
    for k in range(4):
        for j in range(4):
            s = slab_at[4 * k + j]

            def add(p, total):
                rhs = jnp.concatenate(
                    [
                        pseudo_ref[pl.ds(pl.multiple_of(ao[2 * p + h] * 128, 128), 128), :]
                        for h in range(2)
                    ],
                    axis=0,
                )
                return total + jnp.dot(tri_ref[p], rhs, preferred_element_type=jnp.float32)

            total = lax.fori_loop(
                first[s], first[s + 1], add, jnp.zeros((128, pseudo_ref.shape[1]), jnp.float32)
            )
            outs[k][j] = total.astype(jnp.bfloat16)


def slab_sums(first, ao, slab_at, tri_pairs, pseudo):
    cols = pseudo.shape[1]
    piece = jax.ShapeDtypeStruct((4, 128, cols), jnp.bfloat16)
    return pl.pallas_call(
        slab_kernel,
        grid_spec=pltpu.PrefetchScalarGridSpec(
            num_scalar_prefetch=3,
            grid=(1,),
            in_specs=[
                pl.BlockSpec(tri_pairs.shape, lambda i, *_: (0, 0, 0)),
                pl.BlockSpec(pseudo.shape, lambda i, *_: (0, 0)),
            ],
            out_specs=[pl.BlockSpec((4, 128, cols), lambda i, *_: (0, 0, 0))] * 4,
        ),
        out_shape=[piece] * 4,
        compiler_params=pltpu.CompilerParams(vmem_limit_bytes=48 * 1024 * 1024),
        cost_estimate=pl.CostEstimate(
            flops=2 * 40 * 128 * 256 * cols, bytes_accessed=12 * 1024 * 1024, transcendentals=0
        ),
    )(first, ao, slab_at, tri_pairs, pseudo)


def shards(
    coef_occ,
    coef_resp,
    orb_energy,
    lap_index,
    density_mask,
    tri_blocks,
    block_ao,
    block_slab,
    metric,
):
    row, col = lax.axis_index("row"), lax.axis_index("col")
    y, x, core = row // 2, row % 2, col % 2
    t_point = 0.04 * jnp.exp(0.5 * math.log(2.0) * lap_index[0].astype(jnp.float32))
    weighted = (coef_occ.astype(jnp.float32) * jnp.exp(t_point * orb_energy)[None, :]).astype(
        jnp.bfloat16
    )
    w_all = lax.all_gather(weighted.T, "col", axis=0, tiled=True)

    mine = coef_resp.T
    other = send(mine, flip_x)
    depth = mine.shape[0]
    r_all = jnp.zeros((N_ROW * depth, mine.shape[1]), mine.dtype)

    def place(r_all, part, step, xx):
        at = (((y + 4 - step) % 4) * 2 + xx) * depth
        return lax.dynamic_update_slice(r_all, part, (at, 0))

    r_all = place(r_all, mine, 0, x)
    for step in (1, 3, 2):
        r_all = place(r_all, send(mine, along_y(step)), step, x)
    r_all = place(r_all, other, 0, 1 - x)
    for step in (1, 3, 2):
        r_all = place(r_all, send(other, along_y(step)), step, 1 - x)

    ao, slab = block_ao[0], block_slab[0]
    n_blocks = slab.shape[0]
    n_pairs = n_blocks // 2 + N_COL
    ids = jnp.arange(n_blocks, dtype=jnp.int32)
    rank = jnp.sum(
        ((slab[None, :] == slab[:, None]) & (ids[None, :] < ids[:, None])).astype(jnp.int32), axis=1
    )
    slabs = jnp.arange(N_COL + 1, dtype=jnp.int32)
    counts = jnp.sum((slab[None, :] == slabs[:N_COL, None]).astype(jnp.int32), axis=1)
    pairs = (counts + 1) // 2
    first = jnp.sum(jnp.where(slabs[None, :N_COL] < slabs[:, None], pairs[None, :], 0), axis=1)
    start = jnp.sum(jnp.where(slabs[None, :N_COL] < slab[:, None], pairs[None, :], 0), axis=1)
    slot = 2 * start + rank
    hit = jnp.arange(2 * n_pairs, dtype=jnp.int32)[:, None] == slot[None, :]
    block_in = jnp.sum(jnp.where(hit, ids[None, :], 0), axis=1)
    ao_in = jnp.sum(jnp.where(hit, ao[None, :], 0), axis=1)
    used = jnp.any(hit, axis=1)
    tri_in = jnp.where(used[:, None, None], tri_blocks[0][block_in], 0)
    tri_pairs = tri_in.reshape(n_pairs, 256, 128).transpose(0, 2, 1)
    order = [
        ((y + k) % 4) * 4 + ((2 * x + core) ^ j) for k in range(4) for j in range(4)
    ]
    slab_at = jnp.stack(order).astype(jnp.int32)

    rows_here = coef_occ.shape[0]
    cols_here = coef_resp.shape[0]
    product = lax.dot_general(
        w_all, r_all, (((0,), (0,)), ((), ())), preferred_element_type=jnp.float32
    )
    mask_rows, mask_cols = density_mask.shape
    masked = (
        product.reshape(mask_rows, 128, mask_cols, 128)
        * density_mask.astype(jnp.float32)[:, None, :, None]
    )
    pseudo = masked.reshape(rows_here, cols_here).astype(jnp.bfloat16)

    pieces = slab_sums(first, ao_in, slab_at, tri_pairs, pseudo)
    total = pieces[0].astype(jnp.float32)
    arrived = [send(pieces[k], along_y(k)) for k in (1, 3, 2)]
    for part in arrived:
        total = total + part.astype(jnp.float32)
    total = total.astype(jnp.bfloat16)
    got = [send(total[j], owner_of(j)) for j in range(4)]
    i = col % 4
    first_half, second_half = [], []
    for j in range(4):
        e = (i ^ j) % 2
        first_half.append(jnp.where(e == 0, got[j], 0).astype(jnp.float32))
        second_half.append(jnp.where(e == 1, got[j], 0).astype(jnp.float32))
    whole = jnp.concatenate([sum(first_half), sum(second_half)], axis=1).astype(jnp.bfloat16)
    grad = lax.dot_general(
        whole, metric, (((0,), (1,)), ((), ())), preferred_element_type=jnp.float32
    )
    return (pseudo, grad.astype(jnp.bfloat16))


def solution(mesh):
    placed = (
        P("row", "col"),
        P("col", "row"),
        P("col"),
        P(),
        P("row", "col"),
        P("row", None, None, None),
        P("row", None),
        P("row", None),
        P("col", None),
    )
    return jax.shard_map(
        shards,
        mesh=mesh,
        in_specs=placed,
        out_specs=(P("row", "col"), P("row", "col")),
        check_vma=False,
    )
```

```python
import math

import jax
import jax.numpy as jnp
from jax import lax
from jax.sharding import PartitionSpec as P

N_ROW = 8
N_COL = 16
BOTH = ("row", "col")
PARTS = 2

SLAB_PAIR = (
    (0, 7, 3, 5, 4, 6, 1, 2),
    (2, 5, 1, 7, 0, 4, 3, 6),
    (7, 3, 4, 2, 6, 0, 5, 1),
    (0, 1, 5, 3, 7, 2, 6, 4),
    (6, 4, 2, 0, 1, 3, 5, 7),
    (3, 1, 4, 6, 2, 0, 7, 5),
    (4, 0, 7, 6, 5, 3, 2, 1),
    (5, 6, 2, 0, 4, 1, 7, 3),
    (7, 0, 4, 5, 6, 2, 3, 1),
    (5, 2, 6, 3, 7, 1, 0, 4),
    (1, 4, 3, 6, 2, 7, 0, 5),
    (7, 2, 5, 0, 4, 1, 3, 6),
    (6, 4, 7, 2, 1, 0, 5, 3),
    (0, 3, 2, 1, 7, 5, 6, 4),
    (0, 3, 1, 6, 5, 4, 2, 7),
    (2, 5, 0, 4, 3, 7, 1, 6),
)


def send(x, to):
    pairs = []
    for r in range(N_ROW):
        for c in range(N_COL):
            rr, cc = to(r, c)
            pairs.append((r * N_COL + c, rr * N_COL + cc))
    return lax.ppermute(x, BOTH, pairs)


def along_y(step):
    return lambda r, c: ((r + 2 * step) % N_ROW, c)


def flip_x(r, c):
    return r ^ 1, c


def owner_of(j):
    return lambda r, c: (c // 2, 2 * SLAB_PAIR[c][r] + (j ^ (c % 2)))


def add(*terms):
    total = terms[0].astype(jnp.float32)
    for term in terms[1:]:
        total = total + term.astype(jnp.float32)
    return total.astype(jnp.bfloat16)


def shards(
    coef_occ,
    coef_resp,
    orb_energy,
    lap_index,
    density_mask,
    tri_blocks,
    block_ao,
    block_slab,
    metric,
):
    row, col = lax.axis_index("row"), lax.axis_index("col")
    y, x, core = row // 2, row % 2, col % 2
    t_point = 0.04 * jnp.exp(0.5 * math.log(2.0) * lap_index[0].astype(jnp.float32))
    weighted = (coef_occ.astype(jnp.float32) * jnp.exp(t_point * orb_energy)[None, :]).astype(
        jnp.bfloat16
    )
    w_all = lax.all_gather(weighted.T, "col", axis=0, tiled=True)

    mine = coef_resp.T
    other = send(mine, flip_x)
    depth, cols_here = mine.shape
    width = cols_here // PARTS
    r_all = [jnp.zeros((N_ROW * depth, width), mine.dtype) for _ in range(PARTS)]

    def place(r_all, part, step, xx):
        at = (((y + 4 - step) % 4) * 2 + xx) * depth
        return [
            lax.dynamic_update_slice(whole, part[:, h * width : (h + 1) * width], (at, 0))
            for h, whole in enumerate(r_all)
        ]

    r_all = place(r_all, mine, 0, x)
    for step in (1, 3, 2):
        r_all = place(r_all, send(mine, along_y(step)), step, x)
    r_all = place(r_all, other, 0, 1 - x)
    for step in (1, 3, 2):
        r_all = place(r_all, send(other, along_y(step)), step, 1 - x)

    table = lax.dynamic_slice(jnp.asarray(SLAB_PAIR, jnp.int32), (col, 0), (1, N_ROW))[0]
    here = jnp.arange(N_COL, dtype=jnp.int32)
    pair_at = jnp.sum(
        jnp.where(
            jnp.arange(N_ROW, dtype=jnp.int32)[None, :]
            == (((y + here // 4) % 4) * 2 + (x + here // 2 % 2) % 2)[:, None],
            table[None, :],
            0,
        ),
        axis=1,
    )
    slab_at = 2 * pair_at + ((here % 2) ^ core)
    n_ao = coef_occ.shape[0] // 128
    chosen = (block_slab[0][None, None, :] == slab_at[:, None, None]) & (
        block_ao[0][None, None, :] == jnp.arange(n_ao, dtype=jnp.int32)[None, :, None]
    )
    blocks = jnp.einsum(
        "sab,bqm->saqm",
        chosen.astype(jnp.bfloat16),
        tri_blocks[0].transpose(0, 2, 1),
        preferred_element_type=jnp.float32,
    ).astype(jnp.bfloat16)
    matrix = blocks.transpose(0, 2, 1, 3).reshape(N_COL * 128, n_ao * 128)

    rows_here = coef_occ.shape[0]
    mask = density_mask.astype(jnp.float32)
    mask_cols = mask.shape[1] // PARTS
    pseudo, grads = [], []
    for h in range(PARTS):
        r_part = r_all[h]
        if h:
            r_part, low_far, high_far = lax.optimization_barrier((r_part, low_far, high_far))
        product = lax.dot_general(
            w_all, r_part, (((0,), (0,)), ((), ())), preferred_element_type=jnp.float32
        )
        masked = (
            product.reshape(n_ao, 128, mask_cols, 128)
            * mask[:, None, h * mask_cols : (h + 1) * mask_cols, None]
        )
        part = masked.reshape(rows_here, width).astype(jnp.bfloat16)
        pseudo.append(part)

        piece = [None] * 8
        for n in (4, 5, 3, 6, 2, 7, 1, 0):
            piece[n] = jnp.dot(
                matrix[n * 256 : (n + 1) * 256], part, preferred_element_type=jnp.float32
            ).astype(jnp.bfloat16)
        low_far = send(piece[4], along_y(1))
        high_far = send(piece[5], along_y(-1))
        high_up = send(piece[3], along_y(1))
        low_down = send(piece[6], along_y(-1))
        high_down = send(add(piece[7], high_far), along_y(-1))
        low_up = send(add(piece[2], low_far), along_y(1))
        crossed = send(add(piece[1], high_up, high_down), flip_x)
        total = [
            add(piece[0][128 * j : 128 * j + 128], low_down[128 * j : 128 * j + 128],
                low_up[128 * j : 128 * j + 128], crossed[128 * j : 128 * j + 128])
            for j in range(2)
        ]
        got = [send(total[j], owner_of(j)) for j in range(2)]
        grads.append(
            [
                lax.dot_general(
                    jnp.where(core == 0, got[e], got[1 - e]),
                    metric,
                    (((0,), (1,)), ((), ())),
                    preferred_element_type=jnp.float32,
                ).astype(jnp.bfloat16)
                for e in range(2)
            ]
        )
    pseudo, low_far = lax.optimization_barrier((pseudo, low_far))
    grad = jnp.concatenate([grads[h][e] for e in range(2) for h in range(PARTS)], axis=0)
    return (jnp.concatenate(pseudo, axis=1), grad)


def solution(mesh):
    placed = (
        P("row", "col"),
        P("col", "row"),
        P("col"),
        P(),
        P("row", "col"),
        P("row", None, None, None),
        P("row", None),
        P("row", None),
        P("col", None),
    )
    return jax.shard_map(
        shards,
        mesh=mesh,
        in_specs=placed,
        out_specs=(P("row", "col"), P("row", "col")),
        check_vma=False,
    )
```

```python
import math

import jax
import jax.numpy as jnp
from jax import lax
from jax.experimental import pallas as pl
from jax.experimental.pallas import tpu as pltpu
from jax.sharding import PartitionSpec as P

N_ROW = 8
N_COL = 16
BOTH = ("row", "col")
ORDER = (5, 3, 4, 7, 6, 2, 1, 0)

SLAB_PAIR = (
    (3, 5, 1, 4, 0, 7, 2, 6),
    (3, 6, 2, 7, 0, 5, 1, 4),
    (1, 4, 3, 6, 0, 2, 7, 5),
    (5, 0, 7, 2, 4, 6, 3, 1),
    (2, 1, 3, 0, 4, 5, 7, 6),
    (5, 4, 7, 6, 2, 3, 1, 0),
    (0, 3, 4, 6, 5, 2, 7, 1),
    (4, 3, 7, 1, 2, 0, 5, 6),
    (4, 2, 5, 0, 6, 3, 7, 1),
    (5, 0, 4, 2, 6, 3, 7, 1),
    (4, 7, 5, 6, 2, 1, 0, 3),
    (1, 0, 3, 2, 5, 7, 4, 6),
    (3, 4, 5, 1, 2, 0, 7, 6),
    (1, 2, 6, 7, 3, 5, 4, 0),
    (4, 5, 2, 0, 1, 7, 3, 6),
    (3, 6, 1, 5, 4, 7, 2, 0),
)


def send(x, to):
    pairs = []
    for r in range(N_ROW):
        for c in range(N_COL):
            rr, cc = to(r, c)
            pairs.append((r * N_COL + c, rr * N_COL + cc))
    return lax.ppermute(x, BOTH, pairs)


def along_y(step):
    return lambda r, c: ((r + 2 * step) % N_ROW, c)


def flip_x(r, c):
    return r ^ 1, c


def owner_of(j):
    return lambda r, c: (c // 2, 2 * SLAB_PAIR[c][r] + (j ^ (c % 2)))


def add(*terms):
    total = terms[0].astype(jnp.float32)
    for term in terms[1:]:
        total = total + term.astype(jnp.float32)
    return total.astype(jnp.bfloat16)


def pieces_kernel(matrix_ref, part_ref, *outs):
    value = jnp.dot(matrix_ref[...], part_ref[...], preferred_element_type=jnp.float32)
    for n, out in enumerate(outs):

        @pl.when(pl.program_id(0) == n)
        def _(out=out):
            out[...] = value.astype(out.dtype)


def pieces_of(matrix, part, first, count):
    depth, width = part.shape
    piece = jax.ShapeDtypeStruct((256, width), jnp.bfloat16)
    return pl.pallas_call(
        pieces_kernel,
        grid=(count,),
        in_specs=[
            pl.BlockSpec((256, depth), lambda i: (first + i, 0)),
            pl.BlockSpec((depth, width), lambda i: (0, 0)),
        ],
        out_specs=[pl.BlockSpec((256, width), lambda i: (0, 0))] * count,
        out_shape=[piece] * count,
        compiler_params=pltpu.CompilerParams(vmem_limit_bytes=16 * 1024 * 1024),
        cost_estimate=pl.CostEstimate(flops=1, bytes_accessed=1, transcendentals=0),
    )(matrix, part)


def shards(
    coef_occ,
    coef_resp,
    orb_energy,
    lap_index,
    density_mask,
    tri_blocks,
    block_ao,
    block_slab,
    metric,
):
    row, col = lax.axis_index("row"), lax.axis_index("col")
    y, x, core = row // 2, row % 2, col % 2
    t_point = 0.04 * jnp.exp(0.5 * math.log(2.0) * lap_index[0].astype(jnp.float32))
    weighted = (coef_occ.astype(jnp.float32) * jnp.exp(t_point * orb_energy)[None, :]).astype(
        jnp.bfloat16
    )
    w_all = lax.all_gather(weighted.T, "col", axis=0, tiled=True)

    mine = coef_resp.T
    other = send(mine, flip_x)
    depth, cols_here = mine.shape
    r_all = jnp.zeros((N_ROW * depth, cols_here), mine.dtype)

    def place(r_all, part, step, xx):
        at = (((y + 4 - step) % 4) * 2 + xx) * depth
        return lax.dynamic_update_slice(r_all, part, (at, 0))

    r_all = place(r_all, mine, 0, x)
    for step in (1, 3, 2):
        r_all = place(r_all, send(mine, along_y(step)), step, x)
    r_all = place(r_all, other, 0, 1 - x)
    for step in (1, 3, 2):
        r_all = place(r_all, send(other, along_y(step)), step, 1 - x)

    table = lax.dynamic_slice(jnp.asarray(SLAB_PAIR, jnp.int32), (col, 0), (1, N_ROW))[0]
    here = 2 * jnp.asarray(ORDER)[jnp.arange(N_COL) // 2] + jnp.arange(N_COL) % 2
    pair_at = jnp.sum(
        jnp.where(
            jnp.arange(N_ROW, dtype=jnp.int32)[None, :]
            == (((y + here // 4) % 4) * 2 + (x + here // 2 % 2) % 2)[:, None],
            table[None, :],
            0,
        ),
        axis=1,
    )
    slab_at = 2 * pair_at + ((here % 2) ^ core)
    n_ao = coef_occ.shape[0] // 128
    chosen = (block_slab[0][None, None, :] == slab_at[:, None, None]) & (
        block_ao[0][None, None, :] == jnp.arange(n_ao, dtype=jnp.int32)[None, :, None]
    )
    blocks = jnp.einsum(
        "sab,bqm->saqm",
        chosen.astype(jnp.bfloat16),
        tri_blocks[0].transpose(0, 2, 1),
        preferred_element_type=jnp.float32,
    ).astype(jnp.bfloat16)
    matrix = blocks.transpose(0, 2, 1, 3).reshape(N_COL * 128, n_ao * 128)

    rows_here = coef_occ.shape[0]
    product = lax.dot_general(
        w_all, r_all, (((0,), (0,)), ((), ())), preferred_element_type=jnp.float32
    )
    masked = (
        product.reshape(n_ao, 128, cols_here // 128, 128)
        * density_mask.astype(jnp.float32)[:, None, :, None]
    )
    pseudo = masked.reshape(rows_here, cols_here).astype(jnp.bfloat16)

    after = lax.optimization_barrier
    part = pseudo
    (piece,) = pieces_of(matrix, part, 0, 1)
    high_far = send(piece, along_y(-1))
    part, piece = after((part, piece))
    (piece,) = pieces_of(matrix, part, 1, 1)
    high_up = send(piece, along_y(1))
    part, piece = after((part, piece))
    low_two, for_high, low_one, for_low, high_own, low_own = pieces_of(matrix, part, 2, 6)
    high_far, high_up = after((high_far, high_up))
    high_near = add(for_high, high_far)
    high_down = send(high_near, along_y(-1))
    low_one, low_two, high_near = after((low_one, low_two, high_near))
    low_far = send(low_two, along_y(1))
    low_down = send(low_one, along_y(-1))
    low_up = send(add(for_low, low_far), along_y(1))
    high = add(high_own, high_up, high_down)
    crossed = send(high, flip_x)
    total = [
        add(*[term[128 * j : 128 * j + 128] for term in (low_own, low_down, low_up, crossed)])
        for j in range(2)
    ]
    got = [send(total[j], owner_of(j)) for j in range(2)]
    grad = jnp.concatenate(
        [
            lax.dot_general(
                jnp.where(core == 0, got[e], got[1 - e]),
                metric,
                (((0,), (1,)), ((), ())),
                preferred_element_type=jnp.float32,
            ).astype(jnp.bfloat16)
            for e in range(2)
        ],
        axis=0,
    )
    return (pseudo, grad)


def solution(mesh):
    placed = (
        P("row", "col"),
        P("col", "row"),
        P("col"),
        P(),
        P("row", "col"),
        P("row", None, None, None),
        P("row", None),
        P("row", None),
        P("col", None),
    )
    return jax.shard_map(
        shards,
        mesh=mesh,
        in_specs=placed,
        out_specs=(P("row", "col"), P("row", "col")),
        check_vma=False,
    )
```

```python
import math

import jax
import jax.numpy as jnp
from jax import lax
from jax.experimental import pallas as pl
from jax.experimental.pallas import tpu as pltpu
from jax.sharding import PartitionSpec as P

N_ROW = 8
N_COL = 16
BOTH = ("row", "col")
ORDER = (5, 3, 4, 7, 6, 2, 1, 0)

SLAB_PAIR = (
    (3, 5, 1, 4, 0, 7, 2, 6),
    (3, 6, 2, 7, 0, 5, 1, 4),
    (1, 4, 3, 6, 0, 2, 7, 5),
    (5, 0, 7, 2, 4, 6, 3, 1),
    (2, 1, 3, 0, 4, 5, 7, 6),
    (5, 4, 7, 6, 2, 3, 1, 0),
    (0, 3, 4, 6, 5, 2, 7, 1),
    (4, 3, 7, 1, 2, 0, 5, 6),
    (4, 2, 5, 0, 6, 3, 7, 1),
    (5, 0, 4, 2, 6, 3, 7, 1),
    (4, 7, 5, 6, 2, 1, 0, 3),
    (1, 0, 3, 2, 5, 7, 4, 6),
    (3, 4, 5, 1, 2, 0, 7, 6),
    (1, 2, 6, 7, 3, 5, 4, 0),
    (4, 5, 2, 0, 1, 7, 3, 6),
    (3, 6, 1, 5, 4, 7, 2, 0),
)


def send(x, to):
    pairs = []
    for r in range(N_ROW):
        for c in range(N_COL):
            rr, cc = to(r, c)
            pairs.append((r * N_COL + c, rr * N_COL + cc))
    return lax.ppermute(x, BOTH, pairs)


def along_y(step):
    return lambda r, c: ((r + 2 * step) % N_ROW, c)


def flip_x(r, c):
    return r ^ 1, c


def owner_of(j):
    return lambda r, c: (c // 2, 2 * SLAB_PAIR[c][r] + (j ^ (c % 2)))


def add(*terms):
    total = terms[0].astype(jnp.float32)
    for term in terms[1:]:
        total = total + term.astype(jnp.float32)
    return total.astype(jnp.bfloat16)


def pieces_kernel(matrix_ref, part_ref, *outs):
    value = jnp.dot(matrix_ref[...], part_ref[...], preferred_element_type=jnp.float32)
    for n, out in enumerate(outs):

        @pl.when(pl.program_id(0) == n)
        def _(out=out):
            out[...] = value.astype(out.dtype)


def pieces_of(matrix, part, first, count, half=None):
    depth, width = part.shape
    if half is not None:
        width = width // 2
    at = half or 0
    piece = jax.ShapeDtypeStruct((256, width), jnp.bfloat16)
    return pl.pallas_call(
        pieces_kernel,
        grid=(count,),
        in_specs=[
            pl.BlockSpec((256, depth), lambda i: (first + i, 0)),
            pl.BlockSpec((depth, width), lambda i: (0, at)),
        ],
        out_specs=[pl.BlockSpec((256, width), lambda i: (0, 0))] * count,
        out_shape=[piece] * count,
        compiler_params=pltpu.CompilerParams(vmem_limit_bytes=16 * 1024 * 1024),
        cost_estimate=pl.CostEstimate(flops=1, bytes_accessed=1, transcendentals=0),
    )(matrix, part)


def weigh_kernel(lap_ref, energy_ref, coef_ref, out_ref):
    depth = coef_ref.shape[0]
    here = lax.broadcasted_iota(jnp.int32, (depth, depth), 0)
    there = lax.broadcasted_iota(jnp.int32, (depth, depth), 1)
    energy = jnp.sum(jnp.where(here == there, energy_ref[...], 0.0), axis=1, keepdims=True)
    lap = jnp.full(energy.shape, lap_ref[0], jnp.int32).astype(jnp.float32)
    scale = jnp.exp(0.04 * jnp.exp(0.5 * math.log(2.0) * lap) * energy)
    out_ref[...] = (coef_ref[...].astype(jnp.float32) * scale).astype(out_ref.dtype)


def weigh(lap_index, orb_energy, coef):
    return pl.pallas_call(
        weigh_kernel,
        in_specs=[
            pl.BlockSpec(memory_space=pltpu.SMEM),
            pl.BlockSpec(memory_space=pltpu.VMEM),
            pl.BlockSpec(memory_space=pltpu.VMEM),
        ],
        out_specs=pl.BlockSpec(memory_space=pltpu.VMEM),
        out_shape=jax.ShapeDtypeStruct(coef.shape, jnp.bfloat16),
        compiler_params=pltpu.CompilerParams(vmem_limit_bytes=60 * 1024 * 1024),
    )(lap_index, orb_energy[None, :], coef)


def shards(
    coef_occ,
    coef_resp,
    orb_energy,
    lap_index,
    density_mask,
    tri_blocks,
    block_ao,
    block_slab,
    metric,
):
    row, col = lax.axis_index("row"), lax.axis_index("col")
    y, x, core = row // 2, row % 2, col % 2
    weighted = weigh(lap_index, orb_energy, coef_occ.T)
    w_all = lax.all_gather(weighted, "col", axis=0, tiled=True)

    mine = coef_resp.T
    other = send(mine, flip_x)
    depth, cols_here = mine.shape
    r_all = jnp.zeros((N_ROW * depth, cols_here), mine.dtype)

    def place(r_all, part, step, xx):
        at = (((y + 4 - step) % 4) * 2 + xx) * depth
        return lax.dynamic_update_slice(r_all, part, (at, 0))

    r_all = place(r_all, mine, 0, x)
    for step in (1, 3, 2):
        r_all = place(r_all, send(mine, along_y(step)), step, x)
    r_all = place(r_all, other, 0, 1 - x)
    for step in (1, 3, 2):
        r_all = place(r_all, send(other, along_y(step)), step, 1 - x)

    table = lax.dynamic_slice(jnp.asarray(SLAB_PAIR, jnp.int32), (col, 0), (1, N_ROW))[0]
    here = 2 * jnp.asarray(ORDER)[jnp.arange(N_COL) // 2] + jnp.arange(N_COL) % 2
    pair_at = jnp.sum(
        jnp.where(
            jnp.arange(N_ROW, dtype=jnp.int32)[None, :]
            == (((y + here // 4) % 4) * 2 + (x + here // 2 % 2) % 2)[:, None],
            table[None, :],
            0,
        ),
        axis=1,
    )
    slab_at = 2 * pair_at + ((here % 2) ^ core)
    n_ao = coef_occ.shape[0] // 128
    chosen = (block_slab[0][None, None, :] == slab_at[:, None, None]) & (
        block_ao[0][None, None, :] == jnp.arange(n_ao, dtype=jnp.int32)[None, :, None]
    )
    blocks = jnp.einsum(
        "sab,bqm->saqm",
        chosen.astype(jnp.bfloat16),
        tri_blocks[0].transpose(0, 2, 1),
        preferred_element_type=jnp.float32,
    ).astype(jnp.bfloat16)
    matrix = blocks.transpose(0, 2, 1, 3).reshape(N_COL * 128, n_ao * 128)

    rows_here = coef_occ.shape[0]
    product = lax.dot_general(
        w_all, r_all, (((0,), (0,)), ((), ())), preferred_element_type=jnp.float32
    )
    masked = (
        product.reshape(n_ao, 128, cols_here // 128, 128)
        * density_mask.astype(jnp.float32)[:, None, :, None]
    )
    pseudo = masked.reshape(rows_here, cols_here).astype(jnp.bfloat16)

    after = lax.optimization_barrier
    part = pseudo

    def chain(part, *args):
        made = pieces_of(matrix, part, *args)
        return after((part, *made))

    part, piece = chain(part, 0, 1, 0)
    high_far_a = send(piece, along_y(-1))
    part, piece = chain(part, 0, 1, 1)
    high_far_b = send(piece, along_y(-1))
    part, piece = chain(part, 1, 1)
    high_up = send(piece, along_y(1))
    part, piece = chain(part, 2, 1, 0)
    low_far_a = send(piece, along_y(1))
    part, piece = chain(part, 2, 1, 1)
    low_far_b = send(piece, along_y(1))
    part, for_high = chain(part, 3, 1)
    part, low_one, for_low = chain(part, 4, 2)
    wide = for_high.shape[1] // 2
    high_near = add(for_high[:, :wide], high_far_a)
    part, high_near = after((part, high_near))
    high_down_a = send(high_near, along_y(-1))
    high_own, low_own = pieces_of(matrix, part, 6, 2)
    high_far_b, high_up, high_own = after((high_far_b, high_up, high_own))
    high_near = add(for_high[:, wide:], high_far_b)
    high_down_b = send(high_near, along_y(-1))
    low_one, high_near, low_far_a = after((low_one, high_near, low_far_a))
    low_down = send(low_one, along_y(-1))
    low_near = [
        add(for_low[:, :wide], low_far_a),
        add(for_low[:, wide:], low_far_b),
    ]
    low_up = [send(part, along_y(1)) for part in low_near]
    high_down_a, high_down_b, *low_near = after((high_down_a, high_down_b, *low_near))
    low_up = jnp.concatenate(low_up, axis=1)
    high_down = jnp.concatenate([high_down_a, high_down_b], axis=1)
    high = add(high_own, high_up, high_down)
    crossed = send(high, flip_x)
    total = [
        add(*[term[128 * j : 128 * j + 128] for term in (low_own, low_down, low_up, crossed)])
        for j in range(2)
    ]
    got = [send(total[j], owner_of(j)) for j in range(2)]
    grad = jnp.concatenate(
        [
            lax.dot_general(
                jnp.where(core == 0, got[e], got[1 - e]),
                metric,
                (((0,), (1,)), ((), ())),
                preferred_element_type=jnp.float32,
            ).astype(jnp.bfloat16)
            for e in range(2)
        ],
        axis=0,
    )
    return (pseudo, grad)


def solution(mesh):
    placed = (
        P("row", "col"),
        P("col", "row"),
        P("col"),
        P(),
        P("row", "col"),
        P("row", None, None, None),
        P("row", None),
        P("row", None),
        P("col", None),
    )
    return jax.shard_map(
        shards,
        mesh=mesh,
        in_specs=placed,
        out_specs=(P("row", "col"), P("row", "col")),
        check_vma=False,
    )
```

```python
import math

import jax
import jax.numpy as jnp
from jax import lax
from jax.experimental import pallas as pl
from jax.experimental.pallas import tpu as pltpu
from jax.sharding import PartitionSpec as P

N_ROW = 8
N_COL = 16
BOTH = ("row", "col")
ORDER = (5, 3, 4, 7, 6, 2, 1, 0)

SLAB_PAIR = (
    (3, 5, 1, 4, 0, 7, 2, 6),
    (3, 6, 2, 7, 0, 5, 1, 4),
    (1, 4, 3, 6, 0, 2, 7, 5),
    (5, 0, 7, 2, 4, 6, 3, 1),
    (2, 1, 3, 0, 4, 5, 7, 6),
    (5, 4, 7, 6, 2, 3, 1, 0),
    (0, 3, 4, 6, 5, 2, 7, 1),
    (4, 3, 7, 1, 2, 0, 5, 6),
    (4, 2, 5, 0, 6, 3, 7, 1),
    (5, 0, 4, 2, 6, 3, 7, 1),
    (4, 7, 5, 6, 2, 1, 0, 3),
    (1, 0, 3, 2, 5, 7, 4, 6),
    (3, 4, 5, 1, 2, 0, 7, 6),
    (1, 2, 6, 7, 3, 5, 4, 0),
    (4, 5, 2, 0, 1, 7, 3, 6),
    (3, 6, 1, 5, 4, 7, 2, 0),
)


def send(x, to):
    pairs = []
    for r in range(N_ROW):
        for c in range(N_COL):
            rr, cc = to(r, c)
            pairs.append((r * N_COL + c, rr * N_COL + cc))
    return lax.ppermute(x, BOTH, pairs)


def along_y(step):
    return lambda r, c: ((r + 2 * step) % N_ROW, c)


def flip_x(r, c):
    return r ^ 1, c


def owner_of(j):
    return lambda r, c: (c // 2, 2 * SLAB_PAIR[c][r] + (j ^ (c % 2)))


def add(*terms):
    total = terms[0].astype(jnp.float32)
    for term in terms[1:]:
        total = total + term.astype(jnp.float32)
    return total.astype(jnp.bfloat16)


def pieces_kernel(matrix_ref, part_ref, *outs):
    value = jnp.dot(matrix_ref[...], part_ref[...], preferred_element_type=jnp.float32)
    for n, out in enumerate(outs):

        @pl.when(pl.program_id(0) == n)
        def _(out=out):
            out[...] = value.astype(out.dtype)


def pieces_of(matrix, part, first, count, half=None):
    depth, width = part.shape
    if half is not None:
        width = width // 2
    at = half or 0
    piece = jax.ShapeDtypeStruct((256, width), jnp.bfloat16)
    return pl.pallas_call(
        pieces_kernel,
        grid=(count,),
        in_specs=[
            pl.BlockSpec((256, depth), lambda i: (first + i, 0)),
            pl.BlockSpec((depth, width), lambda i: (0, at)),
        ],
        out_specs=[pl.BlockSpec((256, width), lambda i: (0, 0))] * count,
        out_shape=[piece] * count,
        compiler_params=pltpu.CompilerParams(vmem_limit_bytes=16 * 1024 * 1024),
        cost_estimate=pl.CostEstimate(flops=1, bytes_accessed=1, transcendentals=0),
    )(matrix, part)


def weigh_kernel(lap_ref, energy_ref, coef_ref, out_ref):
    depth = coef_ref.shape[0]
    here = lax.broadcasted_iota(jnp.int32, (depth, depth), 0)
    there = lax.broadcasted_iota(jnp.int32, (depth, depth), 1)
    energy = jnp.sum(jnp.where(here == there, energy_ref[...], 0.0), axis=1, keepdims=True)
    lap = jnp.full(energy.shape, lap_ref[0], jnp.int32).astype(jnp.float32)
    scale = jnp.exp(0.04 * jnp.exp(0.5 * math.log(2.0) * lap) * energy)
    out_ref[...] = (coef_ref[...].astype(jnp.float32) * scale).astype(out_ref.dtype)


def weigh(lap_index, orb_energy, coef):
    return pl.pallas_call(
        weigh_kernel,
        in_specs=[
            pl.BlockSpec(memory_space=pltpu.SMEM),
            pl.BlockSpec(memory_space=pltpu.VMEM),
            pl.BlockSpec(memory_space=pltpu.VMEM),
        ],
        out_specs=pl.BlockSpec(memory_space=pltpu.VMEM),
        out_shape=jax.ShapeDtypeStruct(coef.shape, jnp.bfloat16),
        compiler_params=pltpu.CompilerParams(vmem_limit_bytes=60 * 1024 * 1024),
    )(lap_index, orb_energy[None, :], coef)


def shards(
    coef_occ,
    coef_resp,
    orb_energy,
    lap_index,
    density_mask,
    tri_blocks,
    block_ao,
    block_slab,
    metric,
):
    row, col = lax.axis_index("row"), lax.axis_index("col")
    y, x, core = row // 2, row % 2, col % 2
    weighted = weigh(lap_index, orb_energy, coef_occ.T)
    w_all = lax.all_gather(weighted, "col", axis=0, tiled=True)

    mine = coef_resp.T
    other = send(mine, flip_x)
    depth, cols_here = mine.shape
    r_all = jnp.zeros((N_ROW * depth, cols_here), mine.dtype)

    def place(r_all, part, step, xx):
        at = (((y + 4 - step) % 4) * 2 + xx) * depth
        return lax.dynamic_update_slice(r_all, part, (at, 0))

    r_all = place(r_all, mine, 0, x)
    for step in (1, 3, 2):
        r_all = place(r_all, send(mine, along_y(step)), step, x)
    r_all = place(r_all, other, 0, 1 - x)
    for step in (1, 3, 2):
        r_all = place(r_all, send(other, along_y(step)), step, 1 - x)

    table = lax.dynamic_slice(jnp.asarray(SLAB_PAIR, jnp.int32), (col, 0), (1, N_ROW))[0]
    here = 2 * jnp.asarray(ORDER)[jnp.arange(N_COL) // 2] + jnp.arange(N_COL) % 2
    pair_at = jnp.sum(
        jnp.where(
            jnp.arange(N_ROW, dtype=jnp.int32)[None, :]
            == (((y + here // 4) % 4) * 2 + (x + here // 2 % 2) % 2)[:, None],
            table[None, :],
            0,
        ),
        axis=1,
    )
    slab_at = 2 * pair_at + ((here % 2) ^ core)
    n_ao = coef_occ.shape[0] // 128
    chosen = (block_slab[0][None, None, :] == slab_at[:, None, None]) & (
        block_ao[0][None, None, :] == jnp.arange(n_ao, dtype=jnp.int32)[None, :, None]
    )
    blocks = jnp.einsum(
        "sab,bqm->saqm",
        chosen.astype(jnp.bfloat16),
        tri_blocks[0].transpose(0, 2, 1),
        preferred_element_type=jnp.float32,
    ).astype(jnp.bfloat16)
    matrix = blocks.transpose(0, 2, 1, 3).reshape(N_COL * 128, n_ao * 128)

    rows_here = coef_occ.shape[0]
    mask = jnp.broadcast_to(
        density_mask.astype(jnp.bfloat16)[:, None, :, None], (n_ao, 128, cols_here // 128, 128)
    ).reshape(rows_here, cols_here)
    product = lax.dot_general(
        w_all, r_all, (((0,), (0,)), ((), ())), preferred_element_type=jnp.float32
    )
    pseudo = (product * mask.astype(jnp.float32)).astype(jnp.bfloat16)

    after = lax.optimization_barrier
    part = pseudo

    def chain(part, *args):
        made = pieces_of(matrix, part, *args)
        return after((part, *made))

    part, piece = chain(part, 0, 1, 0)
    high_far_a = send(piece, along_y(-1))
    part, piece = chain(part, 0, 1, 1)
    high_far_b = send(piece, along_y(-1))
    part, piece = chain(part, 1, 1)
    high_up = send(piece, along_y(1))
    part, piece = chain(part, 2, 1, 0)
    low_far_a = send(piece, along_y(1))
    part, piece = chain(part, 2, 1, 1)
    low_far_b = send(piece, along_y(1))
    part, for_high = chain(part, 3, 1)
    part, low_one, for_low = chain(part, 4, 2)
    wide = for_high.shape[1] // 2
    high_near = add(for_high[:, :wide], high_far_a)
    part, high_near = after((part, high_near))
    high_down_a = send(high_near, along_y(-1))
    high_own, low_own = pieces_of(matrix, part, 6, 2)
    high_far_b, high_up, high_own = after((high_far_b, high_up, high_own))
    high_near = add(for_high[:, wide:], high_far_b)
    high_down_b = send(high_near, along_y(-1))
    low_one, high_near, low_far_a = after((low_one, high_near, low_far_a))
    low_down = send(low_one, along_y(-1))
    low_near = [
        add(for_low[:, :wide], low_far_a),
        add(for_low[:, wide:], low_far_b),
    ]
    low_up = [send(part, along_y(1)) for part in low_near]
    high_down_a, high_down_b, *low_near = after((high_down_a, high_down_b, *low_near))
    low_up = jnp.concatenate(low_up, axis=1)
    high_down = jnp.concatenate([high_down_a, high_down_b], axis=1)
    high = add(high_own, high_up, high_down)
    crossed = send(high, flip_x)
    total = [
        add(*[term[128 * j : 128 * j + 128] for term in (low_own, low_down, low_up, crossed)])
        for j in range(2)
    ]
    got = [send(total[j], owner_of(j)) for j in range(2)]
    grad = jnp.concatenate(
        [
            lax.dot_general(
                jnp.where(core == 0, got[e], got[1 - e]),
                metric,
                (((0,), (1,)), ((), ())),
                preferred_element_type=jnp.float32,
            ).astype(jnp.bfloat16)
            for e in range(2)
        ],
        axis=0,
    )
    return (pseudo, grad)


def solution(mesh):
    placed = (
        P("row", "col"),
        P("col", "row"),
        P("col"),
        P(),
        P("row", "col"),
        P("row", None, None, None),
        P("row", None),
        P("row", None),
        P("col", None),
    )
    return jax.shard_map(
        shards,
        mesh=mesh,
        in_specs=placed,
        out_specs=(P("row", "col"), P("row", "col")),
        check_vma=False,
    )
```
